32 devices in a mesh: row: 8 (over z, y), col: 4 (over x, core).
Axes of the slice: x: 2, y: 2, z: 4, core: 2. Of those that a mesh axis runs over, the one named last changes fastest.
Arguments:
- amplitudes: float32 [16, 16, 25600], P('row', 'col'), as said below
- cycle_int: float32 [16, 16, 25600], P('row', 'col'), as said below
- ladder_int: float32 [4, 1600, 6400], P(None, 'col'), may hold values from -0.078125 to 0.078125
- window: int32 [4, 2], replicated, may hold values from 0 to 3, as said below
Outputs:
- residual: float32 [16, 16, 25600], P('row', 'col')
The draws below stay inside these ranges and needn't reach their ends.
Inputs may be any that keep to these rules, and one draw needn't show every extreme that they name: amplitudes[i,j,a*160+b] == amplitudes[j,i,b*160+a]. cycle_int[k,j,c*160+b] == cycle_int[j,k,b*160+c]. `window`: the 4 pairs are distinct.
All inputs are finite; a program needn't handle non-finite values.
Results may differ from the reference program's by a relative error of at most 0.0001.
Values sent between devices are 32-bit elements; how exact they have to be, the bound alone decides.
No kernel may reach another device: no remote copies, remote signals or barrier semaphores. Data moves between devices by JAX's collectives and lax.ppermute only.
A program may use at most 320 MiB of HBM per device.

```python
import jax
import jax.numpy as jnp
from jax import lax

NIRR = 4
VI = 40
NWIN = 4
O = 16
V = 160


def draw_amplitudes(key, part):
    key = jax.random.fold_in(key, 11)
    base = jax.random.normal(key, (O, O, V, V), jnp.float32) * 0.6
    return ((base + jnp.transpose(base, (1, 0, 3, 2))) * 0.5).reshape(O, O, V * V)


def draw_cycle_int(key, part):
    key = jax.random.fold_in(key, 23)
    base = jax.random.normal(key, (O, O, V, V), jnp.float32)
    sym = (base + jnp.transpose(base, (1, 0, 3, 2))) * (0.5 / (O * V) ** 0.5)
    return sym.reshape(O, O, V * V)


def draw_window(key, part):
    key = jax.random.fold_in(key, 37)
    order = jax.random.permutation(key, NIRR * NIRR)[:NWIN].astype(jnp.int32)
    return jnp.stack([order // NIRR, order % NIRR], axis=1).astype(jnp.int32)


def block_scale(key, shape, cuts, smallest, largest):
    loudness = 1.0
    for dim, parts in cuts:
        draws = jax.random.uniform(jax.random.fold_in(jax.random.fold_in(key, 6), dim), (parts,), jnp.float32, smallest / len(cuts), largest / len(cuts))
        loudness = loudness * jnp.repeat(jnp.exp(draws), shape[dim] // parts).reshape((-1,) + (1,) * (len(shape) - 1 - dim))
    return loudness


def bell_draw(stream_key, shape, width, limit, cuts=(), dtype=jnp.bfloat16):
    array = width * jax.random.normal(stream_key, shape, jnp.float32)
    if cuts:
        array = array * block_scale(stream_key, shape, cuts, -0.22, 0.18)
    return jnp.clip(array, -limit, limit).astype(dtype)


def setup_inputs(seed: int = 0) -> dict:
    streams_of = jax.random.split(jax.random.key(seed), 5)
    return {
        "amplitudes": draw_amplitudes(jax.random.fold_in(streams_of[4], 71), 0),
        "cycle_int": draw_cycle_int(jax.random.fold_in(streams_of[4], 71), 0),
        "ladder_int": bell_draw(streams_of[2], (NWIN, VI * VI, NIRR * VI * VI), (NIRR * VI * VI) ** -0.5, 0.078125, ((1, 4),), jnp.float32),
        "window": draw_window(jax.random.fold_in(streams_of[4], 71), 0),
    }


def reference(amplitudes, cycle_int, ladder_int, window):
    highest = lax.Precision.HIGHEST
    amp_four = amplitudes.reshape(O, O, V, V)
    cycle_four = cycle_int.reshape(O, O, V, V)
    paired = 2.0 * amp_four - jnp.swapaxes(amp_four, 2, 3)
    direct = jnp.einsum("ikac,kjcb->ijab", paired, cycle_four, precision=highest)
    total = direct + jnp.transpose(direct, (1, 0, 3, 2))
    ladder = jnp.zeros_like(amp_four)
    zero = jnp.int32(0)
    for which in range(NWIN):
        first = window[which, 0].astype(jnp.int32)
        second = window[which, 1].astype(jnp.int32)
        pieces = []
        for irrep in range(NIRR):
            other = jnp.bitwise_xor(jnp.bitwise_xor(first, second), jnp.int32(irrep))
            block_in = lax.dynamic_slice(amp_four, (zero, zero, jnp.int32(irrep * VI), (other * VI).astype(jnp.int32)), (O, O, VI, VI))
            pieces.append(block_in.reshape(O * O, VI * VI))
        joined = jnp.concatenate(pieces, axis=1)
        summed = lax.dot_general(joined, ladder_int[which], (((1,), (1,)), ((), ())), precision=highest, preferred_element_type=jnp.float32)
        ladder = lax.dynamic_update_slice(ladder, summed.reshape(O, O, VI, VI), (zero, zero, (first * VI).astype(jnp.int32), (second * VI).astype(jnp.int32)))
    return (total + ladder).reshape(O, O, V * V)
```

```python
import functools

import jax
import jax.numpy as jnp
from jax import lax
from jax.experimental import pallas as pl
from jax.experimental.pallas import tpu as pltpu
from jax.sharding import PartitionSpec as P

NIRR = 4
VI = 40
NWIN = 4
AXES = ("row", "col")


def general(amplitudes, cycle_int, ladder_int, window):
    highest = lax.Precision.HIGHEST
    rows_i, cols_j, flat_pairs = amplitudes.shape
    virtual = NIRR * VI
    sector = VI
    by_rows = lax.all_gather(amplitudes, "col", axis=1, tiled=True)
    total_j = by_rows.shape[1]
    rows_four = by_rows.reshape(rows_i, total_j, virtual, virtual)
    cycle_down = lax.all_gather(cycle_int, "row", axis=0, tiled=True)
    cycle_across = lax.all_gather(cycle_int, "col", axis=1, tiled=True)
    down_four = cycle_down.reshape(cycle_down.shape[0], cols_j, virtual, virtual)
    direct = 2.0 * jnp.einsum(
        "ikac,kjcb->ijab", rows_four, down_four, precision=highest
    ) - jnp.einsum("ikca,kjcb->ijab", rows_four, down_four, precision=highest)
    by_cols = lax.all_gather(amplitudes, "row", axis=0, tiled=True)
    cols_four = by_cols.reshape(by_cols.shape[0], cols_j, virtual, virtual)
    across_four = cycle_across.reshape(rows_i, cycle_across.shape[1], virtual, virtual)
    mirror = 2.0 * jnp.einsum(
        "kjcb,ikac->ijab", cols_four, across_four, precision=highest
    ) - jnp.einsum("kjbc,ikac->ijab", cols_four, across_four, precision=highest)
    zero = jnp.int32(0)
    pair_cols = ladder_int.shape[1]
    blocks_out = []
    for which in range(NWIN):
        first = window[which, 0]
        second = window[which, 1]
        summed = jnp.zeros((rows_i, total_j, pair_cols), jnp.float32)
        for irrep in range(NIRR):
            other = jnp.bitwise_xor(jnp.bitwise_xor(first, second), jnp.int32(irrep))
            block_in = lax.dynamic_slice(
                rows_four,
                (zero, zero, jnp.int32(irrep * sector), other * sector),
                (rows_i, total_j, sector, sector),
            )
            weights = ladder_int[
                which, :, irrep * sector * sector : (irrep + 1) * sector * sector
            ].reshape(pair_cols, sector, sector)
            summed = summed + lax.dot_general(
                block_in,
                weights,
                (((2, 3), (1, 2)), ((), ())),
                precision=highest,
                preferred_element_type=jnp.float32,
            )
        blocks_out.append(summed)
    stacked = jnp.stack(blocks_out, 2)
    returned = lax.all_to_all(stacked, "col", split_axis=1, concat_axis=3, tiled=True)
    ladder = place_ladder(returned, window)
    return (ladder + direct + mirror).reshape(rows_i, cols_j, virtual * virtual)


def place_ladder(returned, window):
    rows_i, cols_j = returned.shape[:2]
    virtual = NIRR * VI
    ladder = jnp.zeros((rows_i, cols_j, virtual, virtual), jnp.float32)
    for which in range(NWIN):
        placed = returned[:, :, which].reshape(rows_i, cols_j, VI, VI)
        ladder = lax.dynamic_update_slice(
            ladder, placed, (0, 0, window[which, 0] * VI, window[which, 1] * VI)
        )
    return ladder


def split(x):
    high = x.astype(jnp.bfloat16)
    low = (x - high.astype(jnp.float32)).astype(jnp.bfloat16)
    return high, low


def dot(a, b):
    return jnp.dot(a, b, preferred_element_type=jnp.float32)


def dot_t(a, b):
    return lax.dot_general(a, b, (((1,), (1,)), ((), ())), preferred_element_type=jnp.float32)


def ladder_kernel(kinds, t_ref, w_ref, out_ref, both):
    parts, _, rows, depth = t_ref.shape
    count = parts * rows

    @pl.when(pl.program_id(1) == 0)
    def _():
        high, low = split(t_ref[...].reshape(count, depth))
        both[0:count, :] = high
        both[count:, :] = low

    high, low = split(w_ref[0])
    wide = dot_t(high, both[...])
    out_ref[0] = wide[:, :count] + wide[:, count:] + dot_t(low, both[0:count, :])


def ladder_part(by_kind, ladder_int, window):
    parts, _, rows, depth = by_kind.shape
    pairs = ladder_int.shape[1]
    step = pairs // 2
    kinds = jnp.bitwise_xor(window[:, 0], window[:, 1])
    return pl.pallas_call(
        ladder_kernel,
        out_shape=jax.ShapeDtypeStruct((NWIN, pairs, parts * rows), jnp.float32),
        grid_spec=pltpu.PrefetchScalarGridSpec(
            num_scalar_prefetch=1,
            grid=(NWIN, pairs // step),
            in_specs=[
                pl.BlockSpec((parts, 1, rows, depth), lambda w, n, s: (0, s[w], 0, 0)),
                pl.BlockSpec((1, step, depth), lambda w, n, s: (w, n, 0)),
            ],
            out_specs=pl.BlockSpec((1, step, parts * rows), lambda w, n, s: (w, n, 0)),
            scratch_shapes=[pltpu.VMEM((2 * parts * rows, depth), jnp.bfloat16)],
        ),
        compiler_params=pltpu.CompilerParams(vmem_limit_bytes=48 * 2**20),
        cost_estimate=pl.CostEstimate(
            flops=6 * NWIN * pairs * depth * parts * rows,
            bytes_accessed=4 * NWIN * pairs * depth,
            transcendentals=0,
        ),
        name="ladder",
    )(kinds, by_kind, ladder_int)


def cycle_kernel(pairs, has_acc, info, *refs):
    out_ref = refs[-1]
    half = refs[1].shape[0]
    total = refs[-2][...] if has_acc else jnp.zeros(out_ref.shape, jnp.float32)
    core = info[0]
    at = 0
    for n, sources in enumerate(pairs):
        u_high, u_low = split(refs[at][0])
        at += 1
        mine, other = refs[at][...], refs[at + 1][...]
        if sources == 2:
            first = info[1 + len(pairs) + n] == 1
            mine = jnp.where(first, mine, refs[at + 2][...])
            other = jnp.where(first, other, refs[at + 3][...])
        at += 2 * sources
        top = jnp.where(core == 0, mine, other)
        low = jnp.where(core == 0, other, mine)
        x_high, x_low = split(jnp.concatenate([top, low], axis=0))
        total = total + dot(u_high, x_high) + dot(u_low, x_high) + dot(u_high, x_low)
    out_ref[...] = total


def cycle_part(core, panel, chunks, acc):
    rows, cols = panel.shape[1:]
    info = jnp.stack(
        [core] + [c[0] for c in chunks] + [c[1] for c in chunks]
    ).astype(jnp.int32)
    args, specs = [], []
    for n, (_, _, sources) in enumerate(chunks):
        args.append(panel)
        specs.append(pl.BlockSpec((1, rows, cols), lambda g, s, n=n: (s[1 + n], 0, 0)))
        for mine, other in sources:
            for x in (mine, other):
                args.append(x)
                specs.append(pl.BlockSpec(x.shape, lambda g, s: (0, 0)))
    if acc is not None:
        args.append(acc)
        specs.append(pl.BlockSpec(acc.shape, lambda g, s: (0, 0)))
    return pl.pallas_call(
        functools.partial(cycle_kernel, tuple(len(c[2]) for c in chunks), acc is not None),
        out_shape=jax.ShapeDtypeStruct((rows, cols), jnp.float32),
        grid_spec=pltpu.PrefetchScalarGridSpec(
            num_scalar_prefetch=1,
            grid=(1,),
            in_specs=specs,
            out_specs=pl.BlockSpec((rows, cols), lambda g, s: (0, 0)),
        ),
        compiler_params=pltpu.CompilerParams(vmem_limit_bytes=48 * 2**20),
        cost_estimate=pl.CostEstimate(
            flops=6 * len(chunks) * rows * cols * cols,
            bytes_accessed=4 * sum(a.size for a in args),
            transcendentals=0,
        ),
        name="cycle",
    )(info, *args)


def merge_kernel(info, direct_ref, first_ref, second_ref, out_ref):
    n = first_ref.shape[1]
    v = out_ref.shape[2]
    flip = info[0] == 1
    left = jnp.where(flip, second_ref[...], first_ref[...])
    right = jnp.where(flip, first_ref[...], second_ref[...])
    full = direct_ref[...] + jnp.concatenate([left, right], axis=1)
    for i in range(out_ref.shape[0]):
        for j in range(out_ref.shape[1]):
            out_ref[i, j] = full[i * v : (i + 1) * v, j * v : (j + 1) * v]


def permutation(rule):
    pairs = []
    for dev in range(32):
        row, col = divmod(dev, 4)
        to = rule(row // 2, row % 2, col // 2, col % 2)
        if to is not None and 0 <= to[0] < 4:
            pairs.append((dev, (to[0] * 2 + to[1]) * 4 + to[2] * 2 + to[3]))
    return pairs


def blocked(amplitudes, cycle_int, ladder_int, window):
    rows_i, cols_j, flat = amplitudes.shape
    v = NIRR * VI
    row, col = lax.axis_index("row"), lax.axis_index("col")
    z, y, x, core = row // 2, row % 2, col // 2, col % 2

    send = lambda a, rule: lax.ppermute(a, AXES, permutation(rule))
    swap = lambda a: send(a, lambda z, y, x, k: (z, y, x, 1 - k))
    up = lambda a: send(a, lambda z, y, x, k: (z + 1, y, x, k))
    down = lambda a: send(a, lambda z, y, x, k: (z - 1, y, x, k))

    def matrix(four):
        return jnp.transpose(four, (0, 2, 1, 3)).reshape(rows_i * v, cols_j * v)

    own = send(matrix(cycle_int.reshape(rows_i, cols_j, v, v)), lambda z, y, x, k: (z, k, x, y))
    a1, b1 = up(own), down(own)
    a2, b2 = up(a1), down(b1)
    a3, b3 = up(a2), down(b2)

    amp_four = amplitudes.reshape(rows_i, cols_j, v, v)
    paired = matrix(2.0 * amp_four - jnp.swapaxes(amp_four, 2, 3))
    panel = lax.all_gather(paired, "col")
    across = send(panel, lambda z, y, x, k: (z, 1 - y, x, k) if k == y else None)
    panel = jnp.where(core == y, panel, across)

    six = amplitudes.reshape(rows_i * cols_j, NIRR, VI, NIRR, VI)
    kinds = jnp.stack(
        [
            jnp.stack([six[:, c, :, c ^ s, :] for c in range(NIRR)], 1).reshape(
                rows_i * cols_j, NIRR * VI * VI
            )
            for s in range(NIRR)
        ]
    )
    by_kind = lax.all_gather(kinds, "col")
    laddered = ladder_part(by_kind, ladder_int, window)
    pairs = laddered.shape[1]
    stacked = jnp.transpose(
        laddered.reshape(NWIN, pairs, 4, rows_i, cols_j), (3, 2, 4, 0, 1)
    ).reshape(rows_i, 4 * cols_j, NWIN, pairs)
    returned = lax.all_to_all(stacked, "col", split_axis=1, concat_axis=3, tiled=True)
    ladder = place_ladder(returned, window).reshape(rows_i, cols_j, flat)

    one = jnp.int32(1)
    acc = cycle_part(core, panel, [(z, one, [(own, swap(own))])], None)
    acc = cycle_part(
        core,
        panel,
        [
            (jnp.maximum(z - 1, 0), one, [(a1, swap(a1))]),
            (jnp.minimum(z + 1, 3), one, [(b1, swap(b1))]),
        ],
        acc,
    )
    above = (z < 2).astype(jnp.int32)
    acc = cycle_part(
        core,
        panel,
        [(jnp.bitwise_xor(z, 2), above, [(b2, swap(b2)), (a2, swap(a2))])],
        acc,
    )
    acc = cycle_part(
        core,
        panel,
        [(3 - z, above, [(b3, swap(b3)), (a3, swap(a3))])],
        acc,
    )
    direct = send(acc, lambda z, y, x, k: (z, k, x, y))
    turned = acc.T
    half = turned.shape[0] // 2
    same = lax.dynamic_slice(turned, (core * half, 0), (half, half))
    cross = lax.dynamic_slice(turned, ((1 - core) * half, 0), (half, half))
    first = send(same, lambda z, y, x, k: (2 * x + y, k, z // 2, z % 2))
    second = send(cross, lambda z, y, x, k: (2 * x + y, 1 - k, z // 2, z % 2))
    merged = pl.pallas_call(
        merge_kernel,
        out_shape=jax.ShapeDtypeStruct((rows_i, cols_j, v, v), jnp.float32),
        in_specs=[pl.BlockSpec(memory_space=pltpu.SMEM)]
        + [pl.BlockSpec(memory_space=pltpu.VMEM)] * 3,
        out_specs=pl.BlockSpec(memory_space=pltpu.VMEM),
        compiler_params=pltpu.CompilerParams(vmem_limit_bytes=48 * 2**20),
        name="merge",
    )(y.reshape(1).astype(jnp.int32), direct, first, second)
    return merged.reshape(rows_i, cols_j, flat) + ladder


def solution(mesh):
    placed = (P("row", "col", None), P("row", "col", None), P(None, "col", None), P())

    def on_device(amplitudes, cycle_int, ladder_int, window):
        fits = mesh.shape["row"] == 8 and mesh.shape["col"] == 4
        body = blocked if fits and amplitudes.shape[:2] == (2, 4) else general
        return body(amplitudes, cycle_int, ladder_int, window)

    return jax.shard_map(
        on_device, mesh=mesh, in_specs=placed, out_specs=P("row", "col", None), check_vma=False
    )
```

```python
import functools

import jax
import jax.numpy as jnp
from jax import lax
from jax.experimental import pallas as pl
from jax.experimental.pallas import tpu as pltpu
from jax.sharding import PartitionSpec as P

NIRR = 4
VI = 40
NWIN = 4
AXES = ("row", "col")


def cost(us):
    return pl.CostEstimate(flops=int(us * 1e9), bytes_accessed=int(us * 3e6), transcendentals=0)


def general(amplitudes, cycle_int, ladder_int, window):
    highest = lax.Precision.HIGHEST
    rows_i, cols_j, flat_pairs = amplitudes.shape
    virtual = NIRR * VI
    sector = VI
    by_rows = lax.all_gather(amplitudes, "col", axis=1, tiled=True)
    total_j = by_rows.shape[1]
    rows_four = by_rows.reshape(rows_i, total_j, virtual, virtual)
    cycle_down = lax.all_gather(cycle_int, "row", axis=0, tiled=True)
    cycle_across = lax.all_gather(cycle_int, "col", axis=1, tiled=True)
    down_four = cycle_down.reshape(cycle_down.shape[0], cols_j, virtual, virtual)
    direct = 2.0 * jnp.einsum(
        "ikac,kjcb->ijab", rows_four, down_four, precision=highest
    ) - jnp.einsum("ikca,kjcb->ijab", rows_four, down_four, precision=highest)
    by_cols = lax.all_gather(amplitudes, "row", axis=0, tiled=True)
    cols_four = by_cols.reshape(by_cols.shape[0], cols_j, virtual, virtual)
    across_four = cycle_across.reshape(rows_i, cycle_across.shape[1], virtual, virtual)
    mirror = 2.0 * jnp.einsum(
        "kjcb,ikac->ijab", cols_four, across_four, precision=highest
    ) - jnp.einsum("kjbc,ikac->ijab", cols_four, across_four, precision=highest)
    zero = jnp.int32(0)
    pair_cols = ladder_int.shape[1]
    blocks_out = []
    for which in range(NWIN):
        first = window[which, 0]
        second = window[which, 1]
        summed = jnp.zeros((rows_i, total_j, pair_cols), jnp.float32)
        for irrep in range(NIRR):
            other = jnp.bitwise_xor(jnp.bitwise_xor(first, second), jnp.int32(irrep))
            block_in = lax.dynamic_slice(
                rows_four,
                (zero, zero, jnp.int32(irrep * sector), other * sector),
                (rows_i, total_j, sector, sector),
            )
            weights = ladder_int[
                which, :, irrep * sector * sector : (irrep + 1) * sector * sector
            ].reshape(pair_cols, sector, sector)
            summed = summed + lax.dot_general(
                block_in,
                weights,
                (((2, 3), (1, 2)), ((), ())),
                precision=highest,
                preferred_element_type=jnp.float32,
            )
        blocks_out.append(summed)
    stacked = jnp.stack(blocks_out, 2)
    returned = lax.all_to_all(stacked, "col", split_axis=1, concat_axis=3, tiled=True)
    ladder = place_ladder(returned, window)
    return (ladder + direct + mirror).reshape(rows_i, cols_j, virtual * virtual)


def place_ladder(returned, window):
    rows_i, cols_j = returned.shape[:2]
    virtual = NIRR * VI
    ladder = jnp.zeros((rows_i, cols_j, virtual, virtual), jnp.float32)
    for which in range(NWIN):
        placed = returned[:, :, which].reshape(rows_i, cols_j, VI, VI)
        ladder = lax.dynamic_update_slice(
            ladder, placed, (0, 0, window[which, 0] * VI, window[which, 1] * VI)
        )
    return ladder


def split(x):
    high = x.astype(jnp.bfloat16)
    low = (x - high.astype(jnp.float32)).astype(jnp.bfloat16)
    return high, low


def dot(a, b):
    return jnp.dot(a, b, preferred_element_type=jnp.float32)


def dot_t(a, b):
    return lax.dot_general(a, b, (((1,), (1,)), ((), ())), preferred_element_type=jnp.float32)


def ladder_kernel(info, *refs):
    kinds, w_ref, out_ref, both = refs[:-3], refs[-3], refs[-2], refs[-1]
    rows = kinds[0].shape[1]
    count = rows * len(kinds)

    @pl.when(pl.program_id(1) == 0)
    def _():
        high, low = split(jnp.concatenate([k[0] for k in kinds], axis=0))
        both[0:count, :] = high
        both[count:, :] = low

    high, low = split(w_ref[0])
    wide = dot_t(high, both[...])
    out_ref[0, 0] = (wide[:, :count] + wide[:, count:] + dot_t(low, both[0:count, :])).T


def ladder_part(kinds, ladder_int, window, begin, count):
    _, rows, depth = kinds[0].shape
    total = rows * len(kinds)
    pairs = ladder_int.shape[1]
    step = pairs // 2
    return pl.pallas_call(
        ladder_kernel,
        out_shape=jax.ShapeDtypeStruct((count, pairs // step, total, step), jnp.float32),
        grid_spec=pltpu.PrefetchScalarGridSpec(
            num_scalar_prefetch=1,
            grid=(count, pairs // step),
            in_specs=[pl.BlockSpec((1, rows, depth), lambda w, n, s: (jnp.bitwise_xor(s[w + begin, 0], s[w + begin, 1]), 0, 0))] * len(kinds)
            + [pl.BlockSpec((1, step, depth), lambda w, n, s: (w + begin, n, 0))],
            out_specs=pl.BlockSpec((1, 1, total, step), lambda w, n, s: (w, n, 0, 0)),
            scratch_shapes=[pltpu.VMEM((2 * total, depth), jnp.bfloat16)],
        ),
        compiler_params=pltpu.CompilerParams(vmem_limit_bytes=32 * 2**20),
        cost_estimate=cost(5.5 * count),
        name="ladder",
    )(window, *kinds, ladder_int)


def whole(kernel, name, us, shapes, args, info=None, dtype=jnp.float32):
    def spec(shape):
        return pl.BlockSpec(tuple(shape), lambda g: (0,) * len(shape))

    specs = [spec(a.shape) for a in args]
    if info is not None:
        specs = [pl.BlockSpec(memory_space=pltpu.SMEM)] + specs
        args = (info, *args)
    return pl.pallas_call(
        kernel,
        out_shape=[jax.ShapeDtypeStruct(shape, dtype) for shape in shapes],
        grid=(1,),
        in_specs=specs,
        out_specs=[spec(shape) for shape in shapes],
        compiler_params=pltpu.CompilerParams(vmem_limit_bytes=32 * 2**20),
        cost_estimate=cost(us),
        name=name,
    )(*args)


def place():
    row, col = lax.axis_index("row"), lax.axis_index("col")
    return row // 2, row % 2, col


def sort_kernel(flat_ref, out_ref):
    rows_i, cols_j, flat = flat_ref.shape
    group = 4 * NIRR * VI
    for g in range(flat // group):
        x = flat_ref[:, :, g * group : (g + 1) * group].reshape(rows_i * cols_j, group)
        for d in range(NIRR):
            line = [x[:, (a * NIRR + d) * VI : (a * NIRR + d + 1) * VI] for a in range(4)]
            kind = (g * 4 // VI) ^ d
            out_ref[kind, :, g * 4 * VI : (g + 1) * 4 * VI] = jnp.concatenate(line, axis=1)


def turn_kernel(four_ref, zero_ref, one_ref):
    rows_i, cols_j, v, _ = four_ref.shape
    for g, out_ref in enumerate((zero_ref, one_ref)):
        out_ref[...] = jnp.concatenate(
            [four_ref[k, 2 * h + g].T for h in range(2) for k in range(rows_i)], axis=1
        )


def pair_kernel(four_ref, keep_ref, give_ref):
    rows_i, cols_j, v, _ = four_ref.shape
    halves = []
    for h in range(2):
        line = []
        for k in range(2):
            for i in range(rows_i):
                block = four_ref[i, 2 * h + k]
                line.append(2.0 * block.T - block)
        halves.append(jnp.concatenate(line, axis=1))
    low = place()[1] == 0
    keep_ref[...] = jnp.where(low, halves[0], halves[1])
    give_ref[...] = jnp.where(low, halves[1], halves[0])


def join_kernel(keep_ref, got_ref, out_ref):
    v = keep_ref.shape[0]
    n = keep_ref.shape[1] // 2
    low = place()[1] == 0
    for k in range(2):
        keep, got = keep_ref[:, k * n : (k + 1) * n], got_ref[:, k * n : (k + 1) * n]
        out_ref[k * v : (k + 1) * v, :] = jnp.concatenate(
            [jnp.where(low, keep, got), jnp.where(low, got, keep)], axis=1
        )


def arrange_kernel(*refs):
    sources, (high_ref, low_ref) = refs[:4], refs[4:]
    col = place()[2]
    for rel in range(4):
        at = jnp.bitwise_xor(col, rel)
        high_ref[at], low_ref[at] = split(sources[rel][...])


def cycle_kernel(planes, has_acc, final, *refs):
    refs = list(refs)
    high_ref, low_ref = refs.pop(0), refs.pop(0)
    total = refs.pop(0)[...] if has_acc else None
    z, y, _ = place()
    for plane in planes:
        x = refs.pop(0)[...]
        if plane in ("two", "three"):
            x = jnp.where(z < 2, x, refs.pop(0)[...])
        n = x.shape[1] // 2
        m = 2 * x.shape[0]
        high, low = split(jnp.concatenate([x[:, :n], x[:, n:]], axis=0))
        at = {
            "own": z,
            "below": jnp.maximum(z - 1, 0),
            "above": jnp.minimum(z + 1, 3),
            "two": jnp.bitwise_xor(z, 2),
            "three": 3 - z,
        }[plane]
        u_high, u_low = high_ref[at], low_ref[at]
        wide = dot(jnp.concatenate([high, low], axis=0), u_high)
        part = wide[:m] + wide[m:] + dot(high, u_low)
        total = part if total is None else total + part
    if not final:
        refs.pop(0)[...] = total
        return
    keep_ref, give_ref = refs
    v = total.shape[0] // 2
    n = total.shape[1] // 2
    sides = [
        jnp.concatenate([total[h * v : (h + 1) * v, r * n : (r + 1) * n] for h in range(2)], axis=1)
        for r in range(2)
    ]
    low = y == 0
    keep_ref[...] = jnp.where(low, sides[0], sides[1])
    give_ref[...] = jnp.where(low, sides[1], sides[0])


def cycle_part(high, low, chunks, acc, final):
    args = [high, low] + ([] if acc is None else [acc]) + [x for c in chunks for x in c[1]]
    v, n = chunks[0][1][0].shape
    shapes = [(v, n)] * 2 if final else [(2 * v, n)]
    kernel = functools.partial(cycle_kernel, tuple(c[0] for c in chunks), acc is not None, final)
    return whole(kernel, "cycle", 1 + 1.2 * len(chunks), shapes, args)


def add_kernel(keep_ref, got_ref, total_ref, same_ref, cross_ref):
    total = keep_ref[...] + got_ref[...]
    total_ref[...] = total
    n = total.shape[1] // 2
    low = place()[1] == 0
    same_ref[...] = jnp.where(low, total[:, :n], total[:, n:])
    cross_ref[...] = jnp.where(low, total[:, n:], total[:, :n])


def merge_kernel(window, zero_ref, one_ref, s0_ref, c0_ref, s1_ref, c1_ref, early_ref, late_ref, out_ref):
    rows_i, cols_j, v, _ = out_ref.shape
    low = place()[1] == 0
    totals = zero_ref, one_ref
    for i, (s_ref, c_ref) in enumerate(((s0_ref, c0_ref), (s1_ref, c1_ref))):
        same, cross = s_ref[...], c_ref[...]
        image = jnp.where(low, same, cross), jnp.where(low, cross, same)
        for j in range(cols_j):
            at = ((j // 2) * 2 + i) * v
            turned = totals[j % 2][:, at : at + v].T
            to = (j % 2) * v
            out_ref[i, j] = turned + image[j // 2][:, to : to + v]
    for which in range(NWIN):
        source = (early_ref, late_ref)[which // 2]
        first, second = window[which, 0], window[which, 1]
        rows = pl.ds(pl.multiple_of(first * VI, 8), VI)
        for i in range(rows_i):
            for j in range(cols_j):
                piece = source[which % 2, i, j]
                wide = jnp.concatenate(
                    [jnp.where(second == q, piece, 0.0) for q in range(NIRR)], axis=1
                )
                out_ref[i, j, rows, :] += wide


def permutation(rule):
    pairs = []
    for dev in range(32):
        row, col = divmod(dev, 4)
        to = rule(row // 2, row % 2, col // 2, col % 2)
        if to is not None and 0 <= to[0] < 4:
            pairs.append((dev, (to[0] * 2 + to[1]) * 4 + to[2] * 2 + to[3]))
    return pairs


def blocked(amplitudes, cycle_int, ladder_int, window):
    rows_i, cols_j, flat = amplitudes.shape
    v = NIRR * VI
    col = lax.axis_index("col")
    x, core = col // 2, col % 2
    four = (rows_i, cols_j, v, v)
    slab = (v, cols_j * v)

    def send(a, rule):
        names.append(str(len(names)))
        with jax.named_scope("send" + names[-1]):
            return lax.ppermute(a, AXES, permutation(rule))

    swap = lambda a: send(a, lambda z, y, x, k: (z, y, x, 1 - k))
    swap_x = lambda a: send(a, lambda z, y, x, k: (z, y, 1 - x, k))
    swap_xk = lambda a: send(a, lambda z, y, x, k: (z, y, 1 - x, 1 - k))
    swap_y = lambda a: send(a, lambda z, y, x, k: (z, 1 - y, x, k))
    up = lambda a: send(a, lambda z, y, x, k: (z + 1, y, x, k))
    down = lambda a: send(a, lambda z, y, x, k: (z - 1, y, x, k))
    image = lambda a: send(a, lambda z, y, x, k: (2 * x + k, y, z // 2, z % 2))
    image_y = lambda a: send(a, lambda z, y, x, k: (2 * x + k, 1 - y, z // 2, z % 2))
    names = []
    after = lax.optimization_barrier

    def returned(laddered):
        part = lambda n: laddered[:, :, 8 * n : 8 * n + 8]
        got = jnp.stack([part(0), swap(part(1)), swap_x(part(2)), swap_xk(part(3))])
        got = jnp.where(core == 0, got, jnp.stack([got[1], got[0], got[3], got[2]]))
        got = jnp.where(x == 0, got, jnp.concatenate([got[2:], got[:2]]))
        count = laddered.shape[0]
        return jnp.transpose(got, (1, 3, 0, 2, 4)).reshape(count, rows_i, cols_j, VI, VI)

    def products(own, a1, b1, a2, b2):
        return [("own", [own]), ("below", [a1]), ("above", [b1]), ("two", [b2, a2])]

    def add(keep, got):
        return whole(add_kernel, "add", 1, [slab] + [(v, slab[1] // 2)] * 2, (keep, got))

    x0, x1 = whole(turn_kernel, "turn", 1.5, [slab] * 2, (cycle_int.reshape(four),))
    a10, b10 = up(x0), down(x0)
    a11, b11 = up(x1), down(x1)
    amplitudes, x0, x1 = after((amplitudes, x0, x1))
    keep, give = whole(pair_kernel, "pair", 1.5, [slab] * 2, (amplitudes.reshape(four),))
    got = swap_y(give)
    a10, b10, keep, amplitudes = after((a10, b10, keep, amplitudes))

    a20, b20 = up(a10), down(b10)
    (kinds,) = whole(
        sort_kernel, "sort", 8, [(NIRR, rows_i * cols_j, flat // NIRR)], (amplitudes,)
    )
    a11, b11, got, kinds = after((a11, b11, got, kinds))

    a21, b21 = up(a11), down(b11)
    (u,) = whole(join_kernel, "join", 1, [(rows_i * v, cols_j * v)], (keep, got))
    u_x, u_k = swap_x(u), swap(u)
    a20, b20, u, u_k, kinds = after((a20, b20, u, u_k, kinds))

    a30, b30 = up(a20), down(b20)
    kinds_k = swap(kinds)
    a21, b21, u_x, kinds, kinds_k = after((a21, b21, u_x, kinds, kinds_k))

    a31, b31 = up(a21), down(b21)
    u_xk, kinds_x = swap(u_x), swap_x(kinds)
    high, low = whole(
        arrange_kernel,
        "arrange",
        3,
        [(4, rows_i * v, cols_j * v)] * 2,
        (u, u_k, u_x, u_xk),
        None,
        jnp.bfloat16,
    )
    a30, b30, high, low = after((a30, b30, high, low))

    keep0, give0 = cycle_part(
        high, low, products(x0, a10, b10, a20, b20) + [("three", [b30, a30])], None, True
    )
    high, low, give0 = after((high, low, give0))
    got0 = swap_y(give0)
    (part,) = cycle_part(high, low, products(x1, a11, b11, a21, b21), None, False)
    a31, b31, part, kinds_x = after((a31, b31, part, kinds_x))

    keep1, give1 = cycle_part(high, low, [("three", [b31, a31])], part, True)
    kinds_xk = swap(kinds_x)
    give1, kinds_xk, got0 = after((give1, kinds_xk, got0))
    got1 = swap_y(give1)
    total0, same0, cross0 = add(keep0, got0)
    all_kinds, total0, same0, cross0 = after(((kinds, kinds_k, kinds_x, kinds_xk), total0, same0, cross0))
    same0, cross0 = image(same0), image_y(cross0)
    early = ladder_part(all_kinds, ladder_int, window, 0, 2)
    got1, early, all_kinds = after((got1, early, all_kinds))

    total1, same1, cross1 = add(keep1, got1)
    same1, cross1, total1, all_kinds = after((same1, cross1, total1, all_kinds))
    same1, cross1 = image(same1), image_y(cross1)
    late = ladder_part(all_kinds, ladder_int, window, 2, 2)
    same0, cross0, late = after((same0, cross0, late))
    both = returned(jnp.concatenate([early, late]))
    (merged,) = whole(
        merge_kernel,
        "merge",
        2,
        [four],
        (total0, total1, same0, cross0, same1, cross1, both[:2], both[2:]),
        window,
    )
    return merged.reshape(rows_i, cols_j, flat)


def solution(mesh):
    placed = (P("row", "col", None), P("row", "col", None), P(None, "col", None), P())

    def on_device(amplitudes, cycle_int, ladder_int, window):
        fits = mesh.shape["row"] == 8 and mesh.shape["col"] == 4
        body = blocked if fits and amplitudes.shape[:2] == (2, 4) else general
        return body(amplitudes, cycle_int, ladder_int, window)

    return jax.shard_map(
        on_device, mesh=mesh, in_specs=placed, out_specs=P("row", "col", None), check_vma=False
    )
```

```python
import functools

import jax
import jax.numpy as jnp
from jax import lax
from jax.experimental import pallas as pl
from jax.experimental.pallas import tpu as pltpu
from jax.sharding import PartitionSpec as P

NIRR = 4
VI = 40
NWIN = 4
AXES = ("row", "col")


def cost(us):
    return pl.CostEstimate(flops=int(us * 1e9), bytes_accessed=int(us * 3e6), transcendentals=0)


def general(amplitudes, cycle_int, ladder_int, window):
    highest = lax.Precision.HIGHEST
    rows_i, cols_j, flat_pairs = amplitudes.shape
    virtual = NIRR * VI
    sector = VI
    by_rows = lax.all_gather(amplitudes, "col", axis=1, tiled=True)
    total_j = by_rows.shape[1]
    rows_four = by_rows.reshape(rows_i, total_j, virtual, virtual)
    cycle_down = lax.all_gather(cycle_int, "row", axis=0, tiled=True)
    cycle_across = lax.all_gather(cycle_int, "col", axis=1, tiled=True)
    down_four = cycle_down.reshape(cycle_down.shape[0], cols_j, virtual, virtual)
    direct = 2.0 * jnp.einsum(
        "ikac,kjcb->ijab", rows_four, down_four, precision=highest
    ) - jnp.einsum("ikca,kjcb->ijab", rows_four, down_four, precision=highest)
    by_cols = lax.all_gather(amplitudes, "row", axis=0, tiled=True)
    cols_four = by_cols.reshape(by_cols.shape[0], cols_j, virtual, virtual)
    across_four = cycle_across.reshape(rows_i, cycle_across.shape[1], virtual, virtual)
    mirror = 2.0 * jnp.einsum(
        "kjcb,ikac->ijab", cols_four, across_four, precision=highest
    ) - jnp.einsum("kjbc,ikac->ijab", cols_four, across_four, precision=highest)
    zero = jnp.int32(0)
    pair_cols = ladder_int.shape[1]
    blocks_out = []
    for which in range(NWIN):
        first = window[which, 0]
        second = window[which, 1]
        summed = jnp.zeros((rows_i, total_j, pair_cols), jnp.float32)
        for irrep in range(NIRR):
            other = jnp.bitwise_xor(jnp.bitwise_xor(first, second), jnp.int32(irrep))
            block_in = lax.dynamic_slice(
                rows_four,
                (zero, zero, jnp.int32(irrep * sector), other * sector),
                (rows_i, total_j, sector, sector),
            )
            weights = ladder_int[
                which, :, irrep * sector * sector : (irrep + 1) * sector * sector
            ].reshape(pair_cols, sector, sector)
            summed = summed + lax.dot_general(
                block_in,
                weights,
                (((2, 3), (1, 2)), ((), ())),
                precision=highest,
                preferred_element_type=jnp.float32,
            )
        blocks_out.append(summed)
    stacked = jnp.stack(blocks_out, 2)
    returned = lax.all_to_all(stacked, "col", split_axis=1, concat_axis=3, tiled=True)
    ladder = place_ladder(returned, window)
    return (ladder + direct + mirror).reshape(rows_i, cols_j, virtual * virtual)


def place_ladder(returned, window):
    rows_i, cols_j = returned.shape[:2]
    virtual = NIRR * VI
    ladder = jnp.zeros((rows_i, cols_j, virtual, virtual), jnp.float32)
    for which in range(NWIN):
        placed = returned[:, :, which].reshape(rows_i, cols_j, VI, VI)
        ladder = lax.dynamic_update_slice(
            ladder, placed, (0, 0, window[which, 0] * VI, window[which, 1] * VI)
        )
    return ladder


def split(x):
    high = x.astype(jnp.bfloat16)
    low = (x - high.astype(jnp.float32)).astype(jnp.bfloat16)
    return high, low


def dot(a, b):
    return jnp.dot(a, b, preferred_element_type=jnp.float32)


def dot_t(a, b):
    return lax.dot_general(a, b, (((1,), (1,)), ((), ())), preferred_element_type=jnp.float32)


def ladder_kernel(info, *refs):
    kinds, w_ref, out_ref, both = refs[:-3], refs[-3], refs[-2], refs[-1]
    rows = kinds[0].shape[1]
    count = rows * len(kinds)

    @pl.when(pl.program_id(1) == 0)
    def _():
        high, low = split(jnp.concatenate([k[0] for k in kinds], axis=0))
        both[0:count, :] = high
        both[count:, :] = low

    high, low = split(w_ref[0])
    wide = dot_t(high, both[...])
    out_ref[0, 0] = (wide[:, :count] + wide[:, count:] + dot_t(low, both[0:count, :])).T


def ladder_part(kinds, ladder_int, window, begin, count):
    _, rows, depth = kinds[0].shape
    total = rows * len(kinds)
    pairs = ladder_int.shape[1]
    step = pairs // 2
    return pl.pallas_call(
        ladder_kernel,
        out_shape=jax.ShapeDtypeStruct((count, pairs // step, total, step), jnp.float32),
        grid_spec=pltpu.PrefetchScalarGridSpec(
            num_scalar_prefetch=1,
            grid=(count, pairs // step),
            in_specs=[pl.BlockSpec((1, rows, depth), lambda w, n, s: (jnp.bitwise_xor(s[w + begin, 0], s[w + begin, 1]), 0, 0))] * len(kinds)
            + [pl.BlockSpec((1, step, depth), lambda w, n, s: (w + begin, n, 0))],
            out_specs=pl.BlockSpec((1, 1, total, step), lambda w, n, s: (w, n, 0, 0)),
            scratch_shapes=[pltpu.VMEM((2 * total, depth), jnp.bfloat16)],
        ),
        compiler_params=pltpu.CompilerParams(vmem_limit_bytes=32 * 2**20),
        cost_estimate=cost(5.5 * count),
        name="ladder",
    )(window, *kinds, ladder_int)


def whole(kernel, name, us, shapes, args, info=None, dtype=jnp.float32):
    def spec(shape):
        return pl.BlockSpec(tuple(shape), lambda g: (0,) * len(shape))

    specs = [spec(a.shape) for a in args]
    if info is not None:
        specs = [pl.BlockSpec(memory_space=pltpu.SMEM)] + specs
        args = (info, *args)
    return pl.pallas_call(
        kernel,
        out_shape=[jax.ShapeDtypeStruct(shape, dtype) for shape in shapes],
        grid=(1,),
        in_specs=specs,
        out_specs=[spec(shape) for shape in shapes],
        compiler_params=pltpu.CompilerParams(vmem_limit_bytes=32 * 2**20),
        cost_estimate=cost(us),
        name=name,
    )(*args)


def place():
    row, col = lax.axis_index("row"), lax.axis_index("col")
    return row // 2, row % 2, col


def sort_kernel(flat_ref, out_ref):
    rows_i, cols_j, flat = flat_ref.shape
    group = 4 * NIRR * VI
    for g in range(flat // group):
        x = flat_ref[:, :, g * group : (g + 1) * group].reshape(rows_i * cols_j, group)
        for d in range(NIRR):
            line = [x[:, (a * NIRR + d) * VI : (a * NIRR + d + 1) * VI] for a in range(4)]
            kind = (g * 4 // VI) ^ d
            out_ref[kind, :, g * 4 * VI : (g + 1) * 4 * VI] = jnp.concatenate(line, axis=1)


def turn_kernel(four_ref, out_ref):
    rows_i, cols_j, v, _ = four_ref.shape
    for g in range(2):
        out_ref[g * v : (g + 1) * v, :] = jnp.concatenate(
            [four_ref[k, 2 * h + g].T for h in range(2) for k in range(rows_i)], axis=1
        )


def pair_kernel(four_ref, keep_ref, give_ref):
    rows_i, cols_j, v, _ = four_ref.shape
    halves = []
    for h in range(2):
        line = []
        for k in range(2):
            for i in range(rows_i):
                block = four_ref[i, 2 * h + k]
                line.append(2.0 * block.T - block)
        halves.append(jnp.concatenate(line, axis=1))
    low = place()[1] == 0
    keep_ref[...] = jnp.where(low, halves[0], halves[1])
    give_ref[...] = jnp.where(low, halves[1], halves[0])


def join_kernel(keep_ref, got_ref, out_ref):
    v = keep_ref.shape[0]
    n = keep_ref.shape[1] // 2
    low = place()[1] == 0
    for k in range(2):
        keep, got = keep_ref[:, k * n : (k + 1) * n], got_ref[:, k * n : (k + 1) * n]
        out_ref[k * v : (k + 1) * v, :] = jnp.concatenate(
            [jnp.where(low, keep, got), jnp.where(low, got, keep)], axis=1
        )


def arrange_kernel(*refs):
    sources, (high_ref, low_ref) = refs[:4], refs[4:]
    col = place()[2]
    for rel in range(4):
        at = jnp.bitwise_xor(col, rel)
        high_ref[at], low_ref[at] = split(sources[rel][...])


def cycle_kernel(planes, has_acc, final, *refs):
    refs = list(refs)
    high_ref, low_ref = refs.pop(0), refs.pop(0)
    total = refs.pop(0)[...] if has_acc else None
    z, y, _ = place()
    for plane in planes:
        x = refs.pop(0)[...]
        n = x.shape[1] // 2
        m = 2 * x.shape[0]
        high, low = split(jnp.concatenate([x[:, :n], x[:, n:]], axis=0))
        at = {
            "own": z,
            "below": jnp.maximum(z - 1, 0),
            "above": jnp.minimum(z + 1, 3),
            "two": jnp.bitwise_xor(z, 2),
            "three": 3 - z,
        }[plane]
        u_high, u_low = high_ref[at], low_ref[at]
        wide = dot(jnp.concatenate([high, low], axis=0), u_high)
        part = wide[:m] + wide[m:] + dot(high, u_low)
        total = part if total is None else total + part
    if not final:
        refs.pop(0)[...] = total
        return
    v = total.shape[0] // 4
    n = total.shape[1] // 2
    low = y == 0
    for g in range(2):
        sides = [
            jnp.concatenate(
                [total[(2 * h + g) * v : (2 * h + g + 1) * v, r * n : (r + 1) * n] for h in range(2)],
                axis=1,
            )
            for r in range(2)
        ]
        keep_ref, give_ref = refs[2 * g : 2 * g + 2]
        keep_ref[...] = jnp.where(low, sides[0], sides[1])
        give_ref[...] = jnp.where(low, sides[1], sides[0])


def cycle_part(high, low, chunks, acc, final):
    args = [high, low] + ([] if acc is None else [acc]) + [x for c in chunks for x in c[1]]
    v, n = chunks[0][1][0].shape
    shapes = [(v // 2, n)] * 4 if final else [(2 * v, n)]
    kernel = functools.partial(cycle_kernel, tuple(c[0] for c in chunks), acc is not None, final)
    return whole(kernel, "cycle", 1 + 1.2 * len(chunks), shapes, args)


def add_kernel(keep_ref, got_ref, total_ref, same_ref, cross_ref):
    total = keep_ref[...] + got_ref[...]
    total_ref[...] = total
    v, n = total.shape[0] // 2, total.shape[1] // 2
    sides = [
        jnp.concatenate([total[:v, h * n : (h + 1) * n], total[v:, h * n : (h + 1) * n]], axis=1)
        for h in range(2)
    ]
    low = place()[1] == 0
    same_ref[...] = jnp.where(low, sides[0], sides[1])
    cross_ref[...] = jnp.where(low, sides[1], sides[0])


def merge_kernel(window, zero_ref, one_ref, s0_ref, c0_ref, s1_ref, c1_ref, ladder_ref, out_ref):
    rows_i, cols_j, v, _ = out_ref.shape
    low = place()[1] == 0
    totals = zero_ref, one_ref
    for i, (s_ref, c_ref) in enumerate(((s0_ref, c0_ref), (s1_ref, c1_ref))):
        same, cross = s_ref[...], c_ref[...]
        n = same.shape[1] // 2
        image = [
            jnp.concatenate([part[:, :n], part[:, n:]], axis=0)
            for part in (jnp.where(low, same, cross), jnp.where(low, cross, same))
        ]
        for j in range(cols_j):
            at = ((j // 2) * 2 + i) * v
            turned = totals[j % 2][:, at : at + v].T
            to = (j % 2) * v
            out_ref[i, j] = turned + image[j // 2][:, to : to + v]
    for which in range(NWIN):
        first, second = window[which, 0], window[which, 1]
        rows = pl.ds(pl.multiple_of(first * VI, 8), VI)
        for i in range(rows_i):
            for j in range(cols_j):
                piece = ladder_ref[which, i, j]
                wide = jnp.concatenate(
                    [jnp.where(second == q, piece, 0.0) for q in range(NIRR)], axis=1
                )
                out_ref[i, j, rows, :] += wide


def permutation(rule):
    pairs = []
    for dev in range(32):
        row, col = divmod(dev, 4)
        to = rule(row // 2, row % 2, col // 2, col % 2)
        if to is not None and 0 <= to[0] < 4:
            pairs.append((dev, (to[0] * 2 + to[1]) * 4 + to[2] * 2 + to[3]))
    return pairs


def blocked(amplitudes, cycle_int, ladder_int, window):
    rows_i, cols_j, flat = amplitudes.shape
    v = NIRR * VI
    col = lax.axis_index("col")
    x, core = col // 2, col % 2
    four = (rows_i, cols_j, v, v)
    slab = (v, cols_j * v)

    def send(a, rule):
        names.append(str(len(names)))
        with jax.named_scope("send" + names[-1]):
            return lax.ppermute(a, AXES, permutation(rule))

    swap = lambda a: send(a, lambda z, y, x, k: (z, y, x, 1 - k))
    swap_x = lambda a: send(a, lambda z, y, x, k: (z, y, 1 - x, k))
    swap_xk = lambda a: send(a, lambda z, y, x, k: (z, y, 1 - x, 1 - k))
    swap_y = lambda a: send(a, lambda z, y, x, k: (z, 1 - y, x, k))
    up = lambda a, only: send(a, lambda z, y, x, k: (z + 1, y, x, k) if z in only else None)
    down = lambda a, only: send(a, lambda z, y, x, k: (z - 1, y, x, k) if z in only else None)
    ends = lambda a: send(a, lambda z, y, x, k: ({1: 0, 2: 3}[z], y, x, k) if z in (1, 2) else None)
    image = lambda a: send(a, lambda z, y, x, k: (2 * x + k, y, z // 2, z % 2))
    image_y = lambda a: send(a, lambda z, y, x, k: (2 * x + k, 1 - y, z // 2, z % 2))
    names = []
    after = lax.optimization_barrier

    def returned(laddered):
        part = lambda n: laddered[:, :, 8 * n : 8 * n + 8]
        got = jnp.stack([part(0), swap(part(1)), swap_x(part(2)), swap_xk(part(3))])
        got = jnp.where(core == 0, got, jnp.stack([got[1], got[0], got[3], got[2]]))
        got = jnp.where(x == 0, got, jnp.concatenate([got[2:], got[:2]]))
        count = laddered.shape[0]
        return jnp.transpose(got, (1, 3, 0, 2, 4)).reshape(count, rows_i, cols_j, VI, VI)

    def products(own, a1, b1, c2):
        return [("own", [own]), ("below", [a1]), ("above", [b1]), ("two", [c2])]

    def add(keep, got):
        return whole(add_kernel, "add", 1, [slab] + [(v // 2, slab[1])] * 2, (keep, got))

    def ladder_of(begin, count):
        return ladder_part(all_kinds, ladder_int, window, begin, count)

    (x0,) = whole(turn_kernel, "turn", 1.5, [(rows_i * v, slab[1])], (cycle_int.reshape(four),))
    a1, b1 = up(x0, (0, 1, 2)), down(x0, (1, 2, 3))
    amplitudes, x0 = after((amplitudes, x0))
    keep, give = whole(pair_kernel, "pair", 1.5, [slab] * 2, (amplitudes.reshape(four),))
    got = swap_y(give)
    (kinds,) = whole(
        sort_kernel, "sort", 8, [(NIRR, rows_i * cols_j, flat // NIRR)], (amplitudes,)
    )
    a1, b1, got, kinds = after((a1, b1, got, kinds))

    a2, b2 = up(a1, (1, 2)), down(b1, (1, 2))
    (u,) = whole(join_kernel, "join", 1, [(rows_i * v, cols_j * v)], (keep, got))
    u_x, u_k = swap_x(u), swap(u)
    kinds_k = swap(kinds)
    a2, b2, u_x, u_k, kinds, kinds_k = after((a2, b2, u_x, u_k, kinds, kinds_k))

    c2 = jnp.where(lax.axis_index("row") < 4, b2, a2)
    c3 = ends(c2)
    u_xk, kinds_x = swap(u_x), swap_x(kinds)
    high, low = whole(
        arrange_kernel,
        "arrange",
        3,
        [(4, rows_i * v, cols_j * v)] * 2,
        (u, u_k, u_x, u_xk),
        None,
        jnp.bfloat16,
    )
    (part,) = cycle_part(high, low, products(x0, a1, b1, c2), None, False)
    c3, part, kinds_x = after((c3, part, kinds_x))

    keep0, give0, keep1, give1 = cycle_part(high, low, [("three", [c3])], part, True)
    give0, give1, kinds_x = after((give0, give1, kinds_x))
    got0 = swap_y(give0)
    all_kinds = (kinds, kinds_k, kinds_x, swap(kinds_x))
    early = ladder_of(0, 2)
    got0, early, all_kinds, give1 = after((got0, early, all_kinds, give1))

    total0, same0, cross0 = add(keep0, got0)
    got1 = swap_y(give1)
    same0, cross0 = image(same0), image_y(cross0)
    late = ladder_of(2, 2)
    got1, late = after((got1, late))
    total1, same1, cross1 = add(keep1, got1)
    same1, cross1 = image(same1), image_y(cross1)
    ladder = returned(jnp.concatenate([early, late]))
    (merged,) = whole(
        merge_kernel,
        "merge",
        2,
        [four],
        (total0, total1, same0, cross0, same1, cross1, ladder),
        window,
    )
    return merged.reshape(rows_i, cols_j, flat)


def solution(mesh):
    placed = (P("row", "col", None), P("row", "col", None), P(None, "col", None), P())

    def on_device(amplitudes, cycle_int, ladder_int, window):
        fits = mesh.shape["row"] == 8 and mesh.shape["col"] == 4
        body = blocked if fits and amplitudes.shape[:2] == (2, 4) else general
        return body(amplitudes, cycle_int, ladder_int, window)

    return jax.shard_map(
        on_device, mesh=mesh, in_specs=placed, out_specs=P("row", "col", None), check_vma=False
    )
```

```python
import functools

import jax
import jax.numpy as jnp
from jax import lax
from jax.experimental import pallas as pl
from jax.experimental.pallas import tpu as pltpu
from jax.sharding import PartitionSpec as P

NIRR = 4
VI = 40
NWIN = 4
AXES = ("row", "col")


def cost(us):
    return pl.CostEstimate(flops=int(us * 1e9), bytes_accessed=int(us * 3e6), transcendentals=0)


def general(amplitudes, cycle_int, ladder_int, window):
    highest = lax.Precision.HIGHEST
    rows_i, cols_j, flat_pairs = amplitudes.shape
    virtual = NIRR * VI
    sector = VI
    by_rows = lax.all_gather(amplitudes, "col", axis=1, tiled=True)
    total_j = by_rows.shape[1]
    rows_four = by_rows.reshape(rows_i, total_j, virtual, virtual)
    cycle_down = lax.all_gather(cycle_int, "row", axis=0, tiled=True)
    cycle_across = lax.all_gather(cycle_int, "col", axis=1, tiled=True)
    down_four = cycle_down.reshape(cycle_down.shape[0], cols_j, virtual, virtual)
    direct = 2.0 * jnp.einsum(
        "ikac,kjcb->ijab", rows_four, down_four, precision=highest
    ) - jnp.einsum("ikca,kjcb->ijab", rows_four, down_four, precision=highest)
    by_cols = lax.all_gather(amplitudes, "row", axis=0, tiled=True)
    cols_four = by_cols.reshape(by_cols.shape[0], cols_j, virtual, virtual)
    across_four = cycle_across.reshape(rows_i, cycle_across.shape[1], virtual, virtual)
    mirror = 2.0 * jnp.einsum(
        "kjcb,ikac->ijab", cols_four, across_four, precision=highest
    ) - jnp.einsum("kjbc,ikac->ijab", cols_four, across_four, precision=highest)
    zero = jnp.int32(0)
    pair_cols = ladder_int.shape[1]
    blocks_out = []
    for which in range(NWIN):
        first = window[which, 0]
        second = window[which, 1]
        summed = jnp.zeros((rows_i, total_j, pair_cols), jnp.float32)
        for irrep in range(NIRR):
            other = jnp.bitwise_xor(jnp.bitwise_xor(first, second), jnp.int32(irrep))
            block_in = lax.dynamic_slice(
                rows_four,
                (zero, zero, jnp.int32(irrep * sector), other * sector),
                (rows_i, total_j, sector, sector),
            )
            weights = ladder_int[
                which, :, irrep * sector * sector : (irrep + 1) * sector * sector
            ].reshape(pair_cols, sector, sector)
            summed = summed + lax.dot_general(
                block_in,
                weights,
                (((2, 3), (1, 2)), ((), ())),
                precision=highest,
                preferred_element_type=jnp.float32,
            )
        blocks_out.append(summed)
    stacked = jnp.stack(blocks_out, 2)
    returned = lax.all_to_all(stacked, "col", split_axis=1, concat_axis=3, tiled=True)
    ladder = place_ladder(returned, window)
    return (ladder + direct + mirror).reshape(rows_i, cols_j, virtual * virtual)


def place_ladder(returned, window):
    rows_i, cols_j = returned.shape[:2]
    virtual = NIRR * VI
    ladder = jnp.zeros((rows_i, cols_j, virtual, virtual), jnp.float32)
    for which in range(NWIN):
        placed = returned[:, :, which].reshape(rows_i, cols_j, VI, VI)
        ladder = lax.dynamic_update_slice(
            ladder, placed, (0, 0, window[which, 0] * VI, window[which, 1] * VI)
        )
    return ladder


def split(x):
    high = x.astype(jnp.bfloat16)
    low = (x - high.astype(jnp.float32)).astype(jnp.bfloat16)
    return high, low


def dot(a, b):
    return jnp.dot(a, b, preferred_element_type=jnp.float32)


def dot_t(a, b):
    return lax.dot_general(a, b, (((1,), (1,)), ((), ())), preferred_element_type=jnp.float32)


def ladder_kernel(info, *refs):
    kinds, w_ref, out_ref, both = refs[:-3], refs[-3], refs[-2], refs[-1]
    rows = kinds[0].shape[1]
    count = rows * len(kinds)

    @pl.when(pl.program_id(1) == 0)
    def _():
        high, low = split(jnp.concatenate([k[0] for k in kinds], axis=0))
        both[0:count, :] = high
        both[count:, :] = low

    high, low = split(w_ref[0])
    wide = dot_t(high, both[...])
    out_ref[0, 0] = (wide[:, :count] + wide[:, count:] + dot_t(low, both[0:count, :])).T


def ladder_part(kinds, ladder_int, window, begin, count):
    _, rows, depth = kinds[0].shape
    total = rows * len(kinds)
    pairs = ladder_int.shape[1]
    step = pairs // 2
    return pl.pallas_call(
        ladder_kernel,
        out_shape=jax.ShapeDtypeStruct((count, pairs // step, total, step), jnp.float32),
        grid_spec=pltpu.PrefetchScalarGridSpec(
            num_scalar_prefetch=1,
            grid=(count, pairs // step),
            in_specs=[pl.BlockSpec((1, rows, depth), lambda w, n, s: (jnp.bitwise_xor(s[w + begin, 0], s[w + begin, 1]), 0, 0))] * len(kinds)
            + [pl.BlockSpec((1, step, depth), lambda w, n, s: (w + begin, n, 0))],
            out_specs=pl.BlockSpec((1, 1, total, step), lambda w, n, s: (w, n, 0, 0)),
            scratch_shapes=[pltpu.VMEM((2 * total, depth), jnp.bfloat16)],
        ),
        compiler_params=pltpu.CompilerParams(vmem_limit_bytes=32 * 2**20),
        cost_estimate=cost(5.5 * count),
        name="ladder",
    )(window, *kinds, ladder_int)


def whole(kernel, name, us, shapes, args, info=None, dtype=jnp.float32):
    def spec(shape):
        return pl.BlockSpec(tuple(shape), lambda g: (0,) * len(shape))

    specs = [spec(a.shape) for a in args]
    if info is not None:
        specs = [pl.BlockSpec(memory_space=pltpu.SMEM)] + specs
        args = (info, *args)
    return pl.pallas_call(
        kernel,
        out_shape=[jax.ShapeDtypeStruct(shape, dtype) for shape in shapes],
        grid=(1,),
        in_specs=specs,
        out_specs=[spec(shape) for shape in shapes],
        compiler_params=pltpu.CompilerParams(vmem_limit_bytes=32 * 2**20),
        cost_estimate=cost(us),
        name=name,
    )(*args)


def place():
    row, col = lax.axis_index("row"), lax.axis_index("col")
    return row // 2, row % 2, col


def sort_kernel(flat_ref, out_ref):
    rows_i, cols_j, flat = flat_ref.shape
    group = 4 * NIRR * VI
    for g in range(flat // group):
        x = flat_ref[:, :, g * group : (g + 1) * group].reshape(rows_i * cols_j, group)
        for d in range(NIRR):
            line = [x[:, (a * NIRR + d) * VI : (a * NIRR + d + 1) * VI] for a in range(4)]
            kind = (g * 4 // VI) ^ d
            out_ref[kind, :, g * 4 * VI : (g + 1) * 4 * VI] = jnp.concatenate(line, axis=1)


def turn_kernel(four_ref, out_ref):
    rows_i, cols_j, v, _ = four_ref.shape
    for g in range(2):
        out_ref[g * v : (g + 1) * v, :] = jnp.concatenate(
            [four_ref[k, 2 * h + g].T for h in range(2) for k in range(rows_i)], axis=1
        )


def pair_kernel(four_ref, keep_ref, give_ref):
    rows_i, cols_j, v, _ = four_ref.shape
    halves = []
    for h in range(2):
        line = []
        for k in range(2):
            for i in range(rows_i):
                block = four_ref[i, 2 * h + k]
                line.append(2.0 * block.T - block)
        halves.append(jnp.concatenate(line, axis=1))
    low = place()[1] == 0
    keep_ref[...] = jnp.where(low, halves[0], halves[1])
    give_ref[...] = jnp.where(low, halves[1], halves[0])


def join_kernel(keep_ref, got_ref, out_ref):
    v = keep_ref.shape[0]
    n = keep_ref.shape[1] // 2
    low = place()[1] == 0
    for k in range(2):
        keep, got = keep_ref[:, k * n : (k + 1) * n], got_ref[:, k * n : (k + 1) * n]
        out_ref[k * v : (k + 1) * v, :] = jnp.concatenate(
            [jnp.where(low, keep, got), jnp.where(low, got, keep)], axis=1
        )


def arrange_kernel(*refs):
    sources, (high_ref, low_ref) = refs[:4], refs[4:]
    col = place()[2]
    for rel in range(4):
        at = jnp.bitwise_xor(col, rel)
        high_ref[at], low_ref[at] = split(sources[rel][...])


def cycle_kernel(planes, has_acc, final, *refs):
    refs = list(refs)
    high_ref, low_ref = refs.pop(0), refs.pop(0)
    total = refs.pop(0)[...] if has_acc else None
    z, y, _ = place()
    for plane in planes:
        x = refs.pop(0)[...]
        n = x.shape[1] // 2
        m = 2 * x.shape[0]
        high, low = split(jnp.concatenate([x[:, :n], x[:, n:]], axis=0))
        at = {
            "own": z,
            "below": jnp.maximum(z - 1, 0),
            "above": jnp.minimum(z + 1, 3),
            "two": jnp.bitwise_xor(z, 2),
            "three": 3 - z,
        }[plane]
        u_high, u_low = high_ref[at], low_ref[at]
        wide = dot(jnp.concatenate([high, low], axis=0), u_high)
        part = wide[:m] + wide[m:] + dot(high, u_low)
        total = part if total is None else total + part
    if not final:
        refs.pop(0)[...] = total
        return
    v = total.shape[0] // 4
    n = total.shape[1] // 2
    low = y == 0
    for g in range(2):
        sides = [
            jnp.concatenate(
                [total[(2 * h + g) * v : (2 * h + g + 1) * v, r * n : (r + 1) * n] for h in range(2)],
                axis=1,
            )
            for r in range(2)
        ]
        keep_ref, give_ref = refs[2 * g : 2 * g + 2]
        keep_ref[...] = jnp.where(low, sides[0], sides[1])
        give_ref[...] = jnp.where(low, sides[1], sides[0])


def cycle_part(high, low, chunks, acc, final):
    args = [high, low] + ([] if acc is None else [acc]) + [x for c in chunks for x in c[1]]
    v, n = chunks[0][1][0].shape
    shapes = [(v // 2, n)] * 4 if final else [(2 * v, n)]
    kernel = functools.partial(cycle_kernel, tuple(c[0] for c in chunks), acc is not None, final)
    return whole(kernel, "cycle", 1 + 1.2 * len(chunks), shapes, args)


def add_kernel(keep_ref, got_ref, total_ref, same_ref, cross_ref):
    total = keep_ref[...] + got_ref[...]
    total_ref[...] = total
    v, n = total.shape[0] // 2, total.shape[1] // 2
    sides = [
        jnp.concatenate([total[:v, h * n : (h + 1) * n], total[v:, h * n : (h + 1) * n]], axis=1)
        for h in range(2)
    ]
    low = place()[1] == 0
    same_ref[...] = jnp.where(low, sides[0], sides[1])
    cross_ref[...] = jnp.where(low, sides[1], sides[0])


def merge_kernel(window, zero_ref, one_ref, s0_ref, c0_ref, s1_ref, c1_ref, ladder_ref, out_ref):
    rows_i, cols_j, v, _ = out_ref.shape
    low = place()[1] == 0
    totals = zero_ref, one_ref
    for i, (s_ref, c_ref) in enumerate(((s0_ref, c0_ref), (s1_ref, c1_ref))):
        same, cross = s_ref[...], c_ref[...]
        n = same.shape[1] // 2
        image = [
            jnp.concatenate([part[:, :n], part[:, n:]], axis=0)
            for part in (jnp.where(low, same, cross), jnp.where(low, cross, same))
        ]
        for j in range(cols_j):
            at = ((j // 2) * 2 + i) * v
            turned = totals[j % 2][:, at : at + v].T
            to = (j % 2) * v
            out_ref[i, j] = turned + image[j // 2][:, to : to + v]
    for which in range(NWIN):
        first, second = window[which, 0], window[which, 1]
        rows = pl.ds(pl.multiple_of(first * VI, 8), VI)
        for i in range(rows_i):
            for j in range(cols_j):
                piece = ladder_ref[which, i, j]
                wide = jnp.concatenate(
                    [jnp.where(second == q, piece, 0.0) for q in range(NIRR)], axis=1
                )
                out_ref[i, j, rows, :] += wide


def permutation(rule):
    pairs = []
    for dev in range(32):
        row, col = divmod(dev, 4)
        to = rule(row // 2, row % 2, col // 2, col % 2)
        if to is not None and 0 <= to[0] < 4:
            pairs.append((dev, (to[0] * 2 + to[1]) * 4 + to[2] * 2 + to[3]))
    return pairs


def blocked(amplitudes, cycle_int, ladder_int, window):
    rows_i, cols_j, flat = amplitudes.shape
    v = NIRR * VI
    col = lax.axis_index("col")
    x, core = col // 2, col % 2
    four = (rows_i, cols_j, v, v)
    slab = (v, cols_j * v)

    def send(a, rule):
        names.append(str(len(names)))
        with jax.named_scope("send" + names[-1]):
            return lax.ppermute(a, AXES, permutation(rule))

    swap = lambda a: send(a, lambda z, y, x, k: (z, y, x, 1 - k))
    swap_x = lambda a: send(a, lambda z, y, x, k: (z, y, 1 - x, k))
    swap_xk = lambda a: send(a, lambda z, y, x, k: (z, y, 1 - x, 1 - k))
    swap_y = lambda a: send(a, lambda z, y, x, k: (z, 1 - y, x, k))
    up = lambda a, only: send(a, lambda z, y, x, k: (z + 1, y, x, k) if z in only else None)
    down = lambda a, only: send(a, lambda z, y, x, k: (z - 1, y, x, k) if z in only else None)
    ends = lambda a: send(a, lambda z, y, x, k: ({1: 0, 2: 3}[z], y, x, k) if z in (1, 2) else None)
    image = lambda a: send(a, lambda z, y, x, k: (2 * x + k, y, z // 2, z % 2))
    image_y = lambda a: send(a, lambda z, y, x, k: (2 * x + k, 1 - y, z // 2, z % 2))
    names = []
    after = lax.optimization_barrier

    def returned(laddered):
        part = lambda n: laddered[:, :, 8 * n : 8 * n + 8]
        got = jnp.stack([part(0), swap(part(1)), swap_x(part(2)), swap_xk(part(3))])
        got = jnp.where(core == 0, got, jnp.stack([got[1], got[0], got[3], got[2]]))
        got = jnp.where(x == 0, got, jnp.concatenate([got[2:], got[:2]]))
        count = laddered.shape[0]
        return jnp.transpose(got, (1, 3, 0, 2, 4)).reshape(count, rows_i, cols_j, VI, VI)

    def products(own, a1, b1, c2):
        return [("own", [own]), ("below", [a1]), ("above", [b1]), ("two", [c2])]

    def add(keep, got):
        return whole(add_kernel, "add", 1, [slab] + [(v // 2, slab[1])] * 2, (keep, got))

    def ladder_of(begin, count):
        return ladder_part(all_kinds, ladder_int, window, begin, count)

    (x0,) = whole(turn_kernel, "turn", 1.5, [(rows_i * v, slab[1])], (cycle_int.reshape(four),))
    a1, b1 = up(x0, (0, 1, 2)), down(x0, (1, 2, 3))
    amplitudes, x0 = after((amplitudes, x0))
    keep, give = whole(pair_kernel, "pair", 1.5, [slab] * 2, (amplitudes.reshape(four),))
    amplitudes, give = after((amplitudes, give))
    got = swap_y(give)
    (kinds,) = whole(
        sort_kernel, "sort", 30, [(NIRR, rows_i * cols_j, flat // NIRR)], (amplitudes,)
    )
    kinds_x, kinds_k = swap_x(kinds), swap(kinds)
    a1, b1, got, kinds = after((a1, b1, got, kinds))

    a2, b2 = up(a1, (1, 2)), down(b1, (1, 2))
    (u,) = whole(join_kernel, "join", 1, [(rows_i * v, cols_j * v)], (keep, got))
    u_x, u_k = swap_x(u), swap(u)
    a2, b2, u_k, kinds_x = after((a2, b2, u_k, kinds_x))

    c2 = jnp.where(lax.axis_index("row") < 4, b2, a2)
    c3 = ends(c2)
    u_xk = swap(u_x)
    all_kinds = (kinds, kinds_k, kinds_x, swap(kinds_x))
    high, low = whole(
        arrange_kernel,
        "arrange",
        3,
        [(4, rows_i * v, cols_j * v)] * 2,
        (u, u_k, u_x, u_xk),
        None,
        jnp.bfloat16,
    )
    (part,) = cycle_part(high, low, products(x0, a1, b1, c2), None, False)
    first = ladder_of(0, 1)
    c3, part, first, all_kinds = after((c3, part, first, all_kinds))

    keep0, give0, keep1, give1 = cycle_part(high, low, [("three", [c3])], part, True)
    got0 = swap_y(give0)
    early = ladder_of(1, 2)
    got0, early, all_kinds, give1 = after((got0, early, all_kinds, give1))

    total0, same0, cross0 = add(keep0, got0)
    got1 = swap_y(give1)
    same0, cross0 = image(same0), image_y(cross0)
    late = ladder_of(3, 1)
    got1, late = after((got1, late))
    total1, same1, cross1 = add(keep1, got1)
    same1, cross1 = image(same1), image_y(cross1)
    ladder = returned(jnp.concatenate([first, early, late]))
    (merged,) = whole(
        merge_kernel,
        "merge",
        2,
        [four],
        (total0, total1, same0, cross0, same1, cross1, ladder),
        window,
    )
    return merged.reshape(rows_i, cols_j, flat)


def solution(mesh):
    placed = (P("row", "col", None), P("row", "col", None), P(None, "col", None), P())

    def on_device(amplitudes, cycle_int, ladder_int, window):
        fits = mesh.shape["row"] == 8 and mesh.shape["col"] == 4
        body = blocked if fits and amplitudes.shape[:2] == (2, 4) else general
        return body(amplitudes, cycle_int, ladder_int, window)

    return jax.shard_map(
        on_device, mesh=mesh, in_specs=placed, out_specs=P("row", "col", None), check_vma=False
    )
```

```python
import functools

import jax
import jax.numpy as jnp
from jax import lax
from jax.experimental import pallas as pl
from jax.experimental.pallas import tpu as pltpu
from jax.sharding import PartitionSpec as P

NIRR = 4
VI = 40
NWIN = 4
AXES = ("row", "col")


def cost(us):
    return pl.CostEstimate(flops=int(us * 1e9), bytes_accessed=int(us * 3e6), transcendentals=0)


def general(amplitudes, cycle_int, ladder_int, window):
    highest = lax.Precision.HIGHEST
    rows_i, cols_j, flat_pairs = amplitudes.shape
    virtual = NIRR * VI
    sector = VI
    by_rows = lax.all_gather(amplitudes, "col", axis=1, tiled=True)
    total_j = by_rows.shape[1]
    rows_four = by_rows.reshape(rows_i, total_j, virtual, virtual)
    cycle_down = lax.all_gather(cycle_int, "row", axis=0, tiled=True)
    cycle_across = lax.all_gather(cycle_int, "col", axis=1, tiled=True)
    down_four = cycle_down.reshape(cycle_down.shape[0], cols_j, virtual, virtual)
    direct = 2.0 * jnp.einsum(
        "ikac,kjcb->ijab", rows_four, down_four, precision=highest
    ) - jnp.einsum("ikca,kjcb->ijab", rows_four, down_four, precision=highest)
    by_cols = lax.all_gather(amplitudes, "row", axis=0, tiled=True)
    cols_four = by_cols.reshape(by_cols.shape[0], cols_j, virtual, virtual)
    across_four = cycle_across.reshape(rows_i, cycle_across.shape[1], virtual, virtual)
    mirror = 2.0 * jnp.einsum(
        "kjcb,ikac->ijab", cols_four, across_four, precision=highest
    ) - jnp.einsum("kjbc,ikac->ijab", cols_four, across_four, precision=highest)
    zero = jnp.int32(0)
    pair_cols = ladder_int.shape[1]
    blocks_out = []
    for which in range(NWIN):
        first = window[which, 0]
        second = window[which, 1]
        summed = jnp.zeros((rows_i, total_j, pair_cols), jnp.float32)
        for irrep in range(NIRR):
            other = jnp.bitwise_xor(jnp.bitwise_xor(first, second), jnp.int32(irrep))
            block_in = lax.dynamic_slice(
                rows_four,
                (zero, zero, jnp.int32(irrep * sector), other * sector),
                (rows_i, total_j, sector, sector),
            )
            weights = ladder_int[
                which, :, irrep * sector * sector : (irrep + 1) * sector * sector
            ].reshape(pair_cols, sector, sector)
            summed = summed + lax.dot_general(
                block_in,
                weights,
                (((2, 3), (1, 2)), ((), ())),
                precision=highest,
                preferred_element_type=jnp.float32,
            )
        blocks_out.append(summed)
    stacked = jnp.stack(blocks_out, 2)
    returned = lax.all_to_all(stacked, "col", split_axis=1, concat_axis=3, tiled=True)
    ladder = place_ladder(returned, window)
    return (ladder + direct + mirror).reshape(rows_i, cols_j, virtual * virtual)


def place_ladder(returned, window):
    rows_i, cols_j = returned.shape[:2]
    virtual = NIRR * VI
    ladder = jnp.zeros((rows_i, cols_j, virtual, virtual), jnp.float32)
    for which in range(NWIN):
        placed = returned[:, :, which].reshape(rows_i, cols_j, VI, VI)
        ladder = lax.dynamic_update_slice(
            ladder, placed, (0, 0, window[which, 0] * VI, window[which, 1] * VI)
        )
    return ladder


def split(x):
    high = x.astype(jnp.bfloat16)
    low = (x - high.astype(jnp.float32)).astype(jnp.bfloat16)
    return high, low


def dot(a, b):
    return jnp.dot(a, b, preferred_element_type=jnp.float32)


def dot_t(a, b):
    return lax.dot_general(a, b, (((1,), (1,)), ((), ())), preferred_element_type=jnp.float32)


def ladder_kernel(info, *refs):
    kinds, w_ref, out_ref, both = refs[:-3], refs[-3], refs[-2], refs[-1]
    rows = kinds[0].shape[1]
    count = rows * len(kinds)

    @pl.when(pl.program_id(1) == 0)
    def _():
        high, low = split(jnp.concatenate([k[0] for k in kinds], axis=0))
        both[0:count, :] = high
        both[count:, :] = low

    high, low = split(w_ref[0])
    wide = dot_t(high, both[...])
    out_ref[0, 0] = (wide[:, :count] + wide[:, count:] + dot_t(low, both[0:count, :])).T


def ladder_part(kinds, ladder_int, window, begin, count):
    _, rows, depth = kinds[0].shape
    total = rows * len(kinds)
    pairs = ladder_int.shape[1]
    step = pairs // 2
    return pl.pallas_call(
        ladder_kernel,
        out_shape=jax.ShapeDtypeStruct((count, pairs // step, total, step), jnp.float32),
        grid_spec=pltpu.PrefetchScalarGridSpec(
            num_scalar_prefetch=1,
            grid=(count, pairs // step),
            in_specs=[pl.BlockSpec((1, rows, depth), lambda w, n, s: (jnp.bitwise_xor(s[w + begin, 0], s[w + begin, 1]), 0, 0))] * len(kinds)
            + [pl.BlockSpec((1, step, depth), lambda w, n, s: (w + begin, n, 0))],
            out_specs=pl.BlockSpec((1, 1, total, step), lambda w, n, s: (w, n, 0, 0)),
            scratch_shapes=[pltpu.VMEM((2 * total, depth), jnp.bfloat16)],
        ),
        compiler_params=pltpu.CompilerParams(vmem_limit_bytes=32 * 2**20),
        cost_estimate=cost(5.5 * count),
        name="ladder",
    )(window, *kinds, ladder_int)


def whole(kernel, name, us, shapes, args, info=None, dtype=jnp.float32):
    def spec(shape):
        return pl.BlockSpec(tuple(shape), lambda g: (0,) * len(shape))

    specs = [spec(a.shape) for a in args]
    if info is not None:
        specs = [pl.BlockSpec(memory_space=pltpu.SMEM)] + specs
        args = (info, *args)
    return pl.pallas_call(
        kernel,
        out_shape=[jax.ShapeDtypeStruct(shape, dtype) for shape in shapes],
        grid=(1,),
        in_specs=specs,
        out_specs=[spec(shape) for shape in shapes],
        compiler_params=pltpu.CompilerParams(vmem_limit_bytes=32 * 2**20),
        cost_estimate=cost(us),
        name=name,
    )(*args)


def place():
    row, col = lax.axis_index("row"), lax.axis_index("col")
    return row // 2, row % 2, col


def sort_kernel(flat_ref, out_ref):
    rows_i, cols_j, flat = flat_ref.shape
    group = 4 * NIRR * VI
    for g in range(flat // group):
        x = flat_ref[:, :, g * group : (g + 1) * group].reshape(rows_i * cols_j, group)
        for d in range(NIRR):
            line = [x[:, (a * NIRR + d) * VI : (a * NIRR + d + 1) * VI] for a in range(4)]
            kind = (g * 4 // VI) ^ d
            out_ref[kind, :, g * 4 * VI : (g + 1) * 4 * VI] = jnp.concatenate(line, axis=1)


def turn_kernel(four_ref, out_ref):
    rows_i, cols_j, v, _ = four_ref.shape
    for g in range(2):
        out_ref[g * v : (g + 1) * v, :] = jnp.concatenate(
            [four_ref[k, 2 * h + g].T for h in range(2) for k in range(rows_i)], axis=1
        )


def pair_kernel(four_ref, keep_ref, give_ref):
    rows_i, cols_j, v, _ = four_ref.shape
    halves = []
    for h in range(2):
        line = []
        for k in range(2):
            for i in range(rows_i):
                block = four_ref[i, 2 * h + k]
                line.append(2.0 * block.T - block)
        halves.append(jnp.concatenate(line, axis=1))
    low = place()[1] == 0
    keep_ref[...] = jnp.where(low, halves[0], halves[1])
    give_ref[...] = jnp.where(low, halves[1], halves[0])


def join_kernel(keep_ref, got_ref, out_ref):
    v = keep_ref.shape[0]
    n = keep_ref.shape[1] // 2
    low = place()[1] == 0
    for k in range(2):
        keep, got = keep_ref[:, k * n : (k + 1) * n], got_ref[:, k * n : (k + 1) * n]
        out_ref[k * v : (k + 1) * v, :] = jnp.concatenate(
            [jnp.where(low, keep, got), jnp.where(low, got, keep)], axis=1
        )


def arrange_kernel(*refs):
    sources, (high_ref, low_ref) = refs[:4], refs[4:]
    col = place()[2]
    for rel in range(4):
        at = jnp.bitwise_xor(col, rel)
        high_ref[at], low_ref[at] = split(sources[rel][...])


def cycle_kernel(planes, has_acc, final, *refs):
    refs = list(refs)
    high_ref, low_ref = refs.pop(0), refs.pop(0)
    total = refs.pop(0)[...] if has_acc else None
    z, y, _ = place()
    for plane in planes:
        x = refs.pop(0)[...]
        n = x.shape[1] // 2
        m = 2 * x.shape[0]
        high, low = split(jnp.concatenate([x[:, :n], x[:, n:]], axis=0))
        at = {
            "own": z,
            "below": jnp.maximum(z - 1, 0),
            "above": jnp.minimum(z + 1, 3),
            "two": jnp.bitwise_xor(z, 2),
            "three": 3 - z,
        }[plane]
        u_high, u_low = high_ref[at], low_ref[at]
        wide = dot(jnp.concatenate([high, low], axis=0), u_high)
        part = wide[:m] + wide[m:] + dot(high, u_low)
        total = part if total is None else total + part
    if not final:
        refs.pop(0)[...] = total
        return
    v = total.shape[0] // 4
    n = total.shape[1] // 2
    low = y == 0
    for g in range(2):
        sides = [
            jnp.concatenate(
                [total[(2 * h + g) * v : (2 * h + g + 1) * v, r * n : (r + 1) * n] for h in range(2)],
                axis=1,
            )
            for r in range(2)
        ]
        keep_ref, give_ref = refs[2 * g : 2 * g + 2]
        keep_ref[...] = jnp.where(low, sides[0], sides[1])
        give_ref[...] = jnp.where(low, sides[1], sides[0])


def cycle_part(high, low, chunks, acc, final):
    args = [high, low] + ([] if acc is None else [acc]) + [x for c in chunks for x in c[1]]
    v, n = chunks[0][1][0].shape
    shapes = [(v // 2, n)] * 4 if final else [(2 * v, n)]
    kernel = functools.partial(cycle_kernel, tuple(c[0] for c in chunks), acc is not None, final)
    return whole(kernel, "cycle", 1 + 1.2 * len(chunks), shapes, args)


def add_kernel(keep_ref, got_ref, total_ref, same_ref, cross_ref):
    total = keep_ref[...] + got_ref[...]
    total_ref[...] = total
    v, n = total.shape[0] // 2, total.shape[1] // 2
    sides = [
        jnp.concatenate([total[:v, h * n : (h + 1) * n], total[v:, h * n : (h + 1) * n]], axis=1)
        for h in range(2)
    ]
    low = place()[1] == 0
    same_ref[...] = jnp.where(low, sides[0], sides[1])
    cross_ref[...] = jnp.where(low, sides[1], sides[0])


def merge_kernel(window, zero_ref, one_ref, s0_ref, c0_ref, s1_ref, c1_ref, ladder_ref, out_ref):
    rows_i, cols_j, v, _ = out_ref.shape
    low = place()[1] == 0
    totals = zero_ref, one_ref
    for i, (s_ref, c_ref) in enumerate(((s0_ref, c0_ref), (s1_ref, c1_ref))):
        same, cross = s_ref[...], c_ref[...]
        n = same.shape[1] // 2
        image = [
            jnp.concatenate([part[:, :n], part[:, n:]], axis=0)
            for part in (jnp.where(low, same, cross), jnp.where(low, cross, same))
        ]
        for j in range(cols_j):
            at = ((j // 2) * 2 + i) * v
            turned = totals[j % 2][:, at : at + v].T
            to = (j % 2) * v
            out_ref[i, j] = turned + image[j // 2][:, to : to + v]
    for which in range(NWIN):
        first, second = window[which, 0], window[which, 1]
        rows = pl.ds(pl.multiple_of(first * VI, 8), VI)
        for i in range(rows_i):
            for j in range(cols_j):
                piece = ladder_ref[which, i, j]
                wide = jnp.concatenate(
                    [jnp.where(second == q, piece, 0.0) for q in range(NIRR)], axis=1
                )
                out_ref[i, j, rows, :] += wide


def permutation(rule):
    pairs = []
    for dev in range(32):
        row, col = divmod(dev, 4)
        to = rule(row // 2, row % 2, col // 2, col % 2)
        if to is not None and 0 <= to[0] < 4:
            pairs.append((dev, (to[0] * 2 + to[1]) * 4 + to[2] * 2 + to[3]))
    return pairs


def blocked(amplitudes, cycle_int, ladder_int, window):
    rows_i, cols_j, flat = amplitudes.shape
    v = NIRR * VI
    col = lax.axis_index("col")
    x, core = col // 2, col % 2
    four = (rows_i, cols_j, v, v)
    slab = (v, cols_j * v)

    def send(a, rule):
        names.append(str(len(names)))
        with jax.named_scope("send" + names[-1]):
            return lax.ppermute(a, AXES, permutation(rule))

    swap = lambda a: send(a, lambda z, y, x, k: (z, y, x, 1 - k))
    swap_x = lambda a: send(a, lambda z, y, x, k: (z, y, 1 - x, k))
    swap_xk = lambda a: send(a, lambda z, y, x, k: (z, y, 1 - x, 1 - k))
    swap_y = lambda a: send(a, lambda z, y, x, k: (z, 1 - y, x, k))
    up = lambda a, only: send(a, lambda z, y, x, k: (z + 1, y, x, k) if z in only else None)
    down = lambda a, only: send(a, lambda z, y, x, k: (z - 1, y, x, k) if z in only else None)
    ends = lambda a: send(a, lambda z, y, x, k: ({1: 0, 2: 3}[z], y, x, k) if z in (1, 2) else None)
    image = lambda a: send(a, lambda z, y, x, k: (2 * x + k, y, z // 2, z % 2))
    image_y = lambda a: send(a, lambda z, y, x, k: (2 * x + k, 1 - y, z // 2, z % 2))
    names = []
    after = lax.optimization_barrier

    def returned(laddered):
        part = lambda n: laddered[:, :, 8 * n : 8 * n + 8]
        got = jnp.stack([part(0), swap(part(1)), swap_x(part(2)), swap_xk(part(3))])
        got = jnp.where(core == 0, got, jnp.stack([got[1], got[0], got[3], got[2]]))
        got = jnp.where(x == 0, got, jnp.concatenate([got[2:], got[:2]]))
        count = laddered.shape[0]
        return jnp.transpose(got, (1, 3, 0, 2, 4)).reshape(count, rows_i, cols_j, VI, VI)

    def products(own, a1, b1, c2):
        return [("own", [own]), ("below", [a1]), ("above", [b1]), ("two", [c2])]

    def add(keep, got):
        return whole(add_kernel, "add", 1, [slab] + [(v // 2, slab[1])] * 2, (keep, got))

    def ladder_of(begin, count):
        return ladder_part(all_kinds, ladder_int, window, begin, count)

    (x0,) = whole(turn_kernel, "turn", 1.5, [(rows_i * v, slab[1])], (cycle_int.reshape(four),))
    a1, b1 = up(x0, (0, 1, 2)), down(x0, (1, 2, 3))
    amplitudes, x0 = after((amplitudes, x0))
    keep, give = whole(pair_kernel, "pair", 1.5, [slab] * 2, (amplitudes.reshape(four),))
    amplitudes, give = after((amplitudes, give))
    got = swap_y(give)
    (kinds,) = whole(
        sort_kernel, "sort", 30, [(NIRR, rows_i * cols_j, flat // NIRR)], (amplitudes,)
    )
    (u,) = whole(join_kernel, "join", 1, [(rows_i * v, cols_j * v)], (keep, got))
    u_x, u_k = swap_x(u), swap(u)
    a1, b1, u, kinds = after((a1, b1, u, kinds))

    a2, b2 = up(a1, (1, 2)), down(b1, (1, 2))
    kinds_x, kinds_k = swap_x(kinds), swap(kinds)
    a2, b2, u_k, kinds_k = after((a2, b2, u_k, kinds_k))

    c2 = jnp.where(lax.axis_index("row") < 4, b2, a2)
    c3 = ends(c2)
    u_xk = swap(u_x)
    all_kinds = (kinds, kinds_k, kinds_x, swap(kinds_x))
    high, low = whole(
        arrange_kernel,
        "arrange",
        3,
        [(4, rows_i * v, cols_j * v)] * 2,
        (u, u_k, u_x, u_xk),
        None,
        jnp.bfloat16,
    )
    (part,) = cycle_part(high, low, products(x0, a1, b1, c2), None, False)
    first = ladder_of(0, 1)
    c3, part, first, all_kinds = after((c3, part, first, all_kinds))

    keep0, give0, keep1, give1 = cycle_part(high, low, [("three", [c3])], part, True)
    got0 = swap_y(give0)
    early = ladder_of(1, 2)
    got0, early, all_kinds, give1 = after((got0, early, all_kinds, give1))

    total0, same0, cross0 = add(keep0, got0)
    got1 = swap_y(give1)
    same0, cross0 = image(same0), image_y(cross0)
    late = ladder_of(3, 1)
    got1, late = after((got1, late))
    total1, same1, cross1 = add(keep1, got1)
    same1, cross1 = image(same1), image_y(cross1)
    ladder = returned(jnp.concatenate([first, early, late]))
    (merged,) = whole(
        merge_kernel,
        "merge",
        2,
        [four],
        (total0, total1, same0, cross0, same1, cross1, ladder),
        window,
    )
    return merged.reshape(rows_i, cols_j, flat)


def solution(mesh):
    placed = (P("row", "col", None), P("row", "col", None), P(None, "col", None), P())

    def on_device(amplitudes, cycle_int, ladder_int, window):
        fits = mesh.shape["row"] == 8 and mesh.shape["col"] == 4
        body = blocked if fits and amplitudes.shape[:2] == (2, 4) else general
        return body(amplitudes, cycle_int, ladder_int, window)

    return jax.shard_map(
        on_device, mesh=mesh, in_specs=placed, out_specs=P("row", "col", None), check_vma=False
    )
```
